32 devices in a mesh: groups: 2 (over x), pair: 16 (over z, y, core).
Axes of the slice: x: 2, y: 2, z: 4, core: 2. Of those that a mesh axis runs over, the one named last changes fastest.
Arguments:
- density: bfloat16 [256, 48, 256], P(('groups', 'pair')), parts along dimension 0, may hold values from -6 to 6
- three_index: bfloat16 [256, 32, 128, 256], P(('groups', 'pair')), parts along dimension 0, may hold values from -0.09375 to 0.09375
- live: int32 [256], P(('groups', 'pair')), parts along dimension 0, may hold values from 1 to 32, as said below
- screen: int32 [256, 32], P(('groups', 'pair')), parts along dimension 0, may hold values from 0 to 31
- metric_inverse: float32 [4096, 4096], P('pair'), as said below
Outputs:
- response: bfloat16 [256, 48, 256], P(('groups', 'pair')), parts along dimension 0
- coefficients: float32 [64, 48, 128], P(('groups', 'pair')), parts along dimension 0
The draws below stay inside these ranges and needn't reach their ends.
There are 2 independent parts, one for each index of `groups`. The reference program is written for one: setup_inputs(seed, part) draws one part's arguments, and reference() takes and returns one part's arrays. A program takes and returns all parts, laid end to end along the dimension named above; an argument that names none is the same for every part. Nothing has to cross between parts.
Inputs may be any that keep to these rules, and one draw needn't show every extreme that they name: `live`: at least one block has all 32 slots in use. `metric_inverse`: lower triangular with a positive diagonal.
All inputs are finite; a program needn't handle non-finite values.
Results may differ from the reference program's by a relative error of at most 0.0049.
Values may be sent and summed in bfloat16 or wider, within the bound.
No kernel may reach another device: no remote copies, remote signals or barrier semaphores. Data moves between devices by JAX's collectives and lax.ppermute only.
A program may use at most 128 MiB of HBM per device.

```python
import math
import jax
import jax.numpy as jnp
import numpy as np
from jax import lax

STATES = 48
AUX_BLK = 128
PAIR_BLK = 256
NSCR = 32
BLK_DEV = 8
NBLK = 128
NAB = 32
AUX = 4096


def draw_live(key, part):
    key = jax.random.fold_in(key, 5)
    first, second = jax.random.split(key)
    factor = jax.random.randint(first, (NBLK // BLK_DEV,), 1, 5)
    base = jax.random.randint(second, (NBLK,), 0, NSCR)
    values = 1 + base * jnp.repeat(factor, BLK_DEV) // 4
    values = jnp.minimum(values, NSCR)
    return values.at[0].set(NSCR).astype(jnp.int32)


def draw_metric_inverse(key, part):
    key = jax.random.fold_in(key, 9)
    first, second = jax.random.split(key)
    rows = lax.broadcasted_iota(jnp.int32, (AUX, AUX), 0)
    cols = lax.broadcasted_iota(jnp.int32, (AUX, AUX), 1)
    below = jax.random.normal(first, (AUX, AUX), jnp.float32) * (0.6 / AUX ** 0.5)
    diagonal = jax.random.uniform(second, (AUX,), jnp.float32, 0.5, 1.5)
    lower = jnp.where(rows > cols, below, 0.0)
    return lower + jnp.where(rows == cols, diagonal[:, None], 0.0)


def set_ends(array, rng, low, high):
    longest = array.shape.index(max(array.shape))
    spots = []
    for shift in (0, 1):
        where = [jax.random.randint(jax.random.fold_in(rng, axis), (), 0, length) for axis, length in enumerate(array.shape)]
        where[longest] = (where[longest] + shift) % array.shape[longest]
        spots.append(tuple(where))
    return array.at[spots[0]].set(low).at[spots[1]].set(high)


def level_of(stream_key, dims, cuts, low, high):
    def one(axis_at, blocks):
        steps = jax.random.uniform(jax.random.fold_in(jax.random.fold_in(stream_key, 6), axis_at), (blocks,), jnp.float32, low / len(cuts), high / len(cuts))
        return jnp.repeat(jnp.exp(steps), dims[axis_at] // blocks).reshape((-1,) + (1,) * (len(dims) - axis_at - 1))

    factor_of = one(*cuts[0])
    for cut in cuts[1:]:
        factor_of = factor_of * one(*cut)
    return factor_of


def cumulative_ranks(count, lean):
    loads = [(1 << 20) // math.isqrt(standing ** lean) + 1 for standing in range(1, count + 1)]
    spread = 1 + sum(loads) // (1 << 30)
    return np.cumsum(np.array([max(1, weight // spread) for weight in loads]))


def skewed_ids(key, shape, number_of, lean):
    grid = cumulative_ranks(number_of, lean)
    lot = jax.random.randint(jax.random.fold_in(key, 1), shape, 0, int(grid[number_of - 1]))
    standing = jnp.searchsorted(jnp.asarray(grid, jnp.int32), lot, side="right")
    return jax.random.permutation(jax.random.fold_in(key, 2), number_of)[standing].astype(jnp.int32)


def bell_draw(key, shape, spread, limit, shards=(), held_as=jnp.bfloat16):
    drawn = spread * jax.random.normal(key, shape, jnp.float32)
    if shards:
        drawn = drawn * level_of(key, shape, shards, -0.22, 0.18)
    return jnp.clip(drawn, -limit, limit).astype(held_as)


def setup_inputs(seed: int = 0, part: int = 0) -> dict:
    streams_of = jax.random.split(jax.random.key(seed), 6)
    part_splits = jax.random.split(jax.random.fold_in(streams_of[5], part), 6)
    return {
        "density": bell_draw(part_splits[0], (NBLK, STATES, PAIR_BLK), 1.0, 6.0, ((0, 16),)),
        "three_index": bell_draw(part_splits[1], (NBLK, NSCR, AUX_BLK, PAIR_BLK), (16 * PAIR_BLK) ** -0.5, 0.09375, ((0, 16),)),
        "live": draw_live(jax.random.fold_in(jax.random.fold_in(streams_of[5], part), 71), part),
        "screen": set_ends(skewed_ids(part_splits[3], (NBLK, NSCR), NAB, 2), jax.random.fold_in(part_splits[3], 3), 0, NAB - 1).astype(jnp.int32),
        "metric_inverse": draw_metric_inverse(jax.random.fold_in(streams_of[5], 71), part),
    }


def reference(density, three_index, live, screen, metric_inverse):
    slots = lax.broadcasted_iota(jnp.int32, screen.shape, 1)
    mask = (slots < live[:, None]).astype(jnp.float32)
    contrib = jnp.einsum("bkrj,bsj->bksr", three_index.astype(jnp.float32), density.astype(jnp.float32))
    contrib = contrib * mask[:, :, None, None]
    gamma = jnp.zeros((NAB, STATES, AUX_BLK), jnp.float32)
    gamma = gamma.at[screen.reshape(-1)].add(contrib.reshape(-1, STATES, AUX_BLK))
    metric = metric_inverse.reshape(NAB, AUX_BLK, NAB, AUX_BLK)
    fitted = jnp.einsum("xrqt,qst->xsr", metric, gamma, precision=lax.Precision.HIGHEST)
    coefficients = jnp.einsum("xrqt,xsr->qst", metric, fitted, precision=lax.Precision.HIGHEST)
    rounded = coefficients.astype(jnp.bfloat16)
    picked = rounded[screen] * mask[:, :, None, None].astype(jnp.bfloat16)
    response = jnp.einsum("bkrj,bksr->bsj", three_index.astype(jnp.float32), picked.astype(jnp.float32))
    return response.astype(jnp.bfloat16), coefficients
```

```python
import functools

import jax
import jax.numpy as jnp
from jax import lax
from jax.experimental import pallas as pl
from jax.experimental.pallas import tpu as pltpu
from jax.sharding import PartitionSpec as P

F32 = jnp.float32
BF16 = jnp.bfloat16
NT = (((1,), (1,)), ((), ()))
NN = (((1,), (0,)), ((), ()))
PAIRS = 8
MIB = 2**20


def row_of(a, own, half, me):
    side = (a // own) % 2
    return jnp.where(side == me, 0, half) + (a // (2 * own)) * own + a % own


def fetch(live_h, screen_h, table_h, live, screen, slots, table, small_sem, table_sem):
    blocks, per_block = screen.shape
    aux = table.shape[0] // (blocks * per_block)
    first = pltpu.make_async_copy(live_h, live, small_sem.at[0])
    second = pltpu.make_async_copy(screen_h, screen, small_sem.at[1])
    first.start()
    second.start()
    first.wait()
    for b in range(blocks):
        block_copy(table_h, table, table_sem, live, b, per_block * aux, aux).start()

    def block(b, total):
        pairs = (live[b] + 1) // 2

        def one(p, _):
            slots[total + p] = b * per_block + 2 * p
            return 0

        lax.fori_loop(0, pairs, one, 0)
        return total + pairs

    total = lax.fori_loop(0, blocks, block, 0)
    for p in range(PAIRS):
        slots[total + p] = 0
    second.wait()
    return total


def block_copy(table_h, table, table_sem, live, b, block_rows, aux):
    rows = pl.multiple_of((live[b] + 1) // 2 * 2 * aux, 2 * aux)
    part = pl.ds(pl.multiple_of(b * block_rows, 2 * aux), rows)
    return pltpu.make_async_copy(table_h.at[part], table.at[part], table_sem.at[b])


def pair_at(i, slots, live, screen, total, dead, own, half, me):
    per_block = screen.shape[1]
    slot = slots[i]
    b, t = slot // per_block, slot % per_block
    rows = [row_of(screen[b, t + k], own, half, me) for k in (0, 1)]
    rows = [jnp.where((i < total) & (t + k < live[b]), rows[k], dead) for k in (0, 1)]
    return slot, b, t, rows


def gamma_kernel(own, axis, live_h, screen_h, density_h, table_h, keep, send, live, screen, slots, density, table, acc, small_sem, table_sem):
    blocks, per_block = screen.shape
    half, states, aux = keep.shape
    me = lax.axis_index(axis) % 2
    third = pltpu.make_async_copy(density_h, density, small_sem.at[2])
    third.start()
    total = fetch(live_h, screen_h, table_h, live, screen, slots, table, small_sem, table_sem)
    acc[...] = jnp.zeros_like(acc)
    third.wait()

    def chunk(c, _):
        results = []
        for p in range(PAIRS):
            i = c * PAIRS + p
            slot, b, t, rows = pair_at(i, slots, live, screen, total, 2 * half, own, half, me)

            @pl.when((t == 0) & (i < total))
            def _():
                block_copy(table_h, table, table_sem, live, b, per_block * aux, aux).wait()

            results.append((slot, b, rows))
        products = []
        for slot, b, rows in results:
            tile = table[pl.ds(pl.multiple_of(slot * aux, 2 * aux), 2 * aux), :]
            products.append(lax.dot_general(density[b], tile, NT, preferred_element_type=F32))
        for (slot, b, rows), product in zip(results, products):
            for k in (0, 1):
                acc[rows[k]] = acc[rows[k]] + product[:, k * aux : (k + 1) * aux]
        return 0

    lax.fori_loop(0, (total + PAIRS - 1) // PAIRS, chunk, 0)
    keep[...] = acc[0:half]
    send[...] = acc[half : 2 * half].astype(send.dtype)


def response_kernel(own, axis, live_h, screen_h, table_h, coef_own, coef_other, out, live, screen, slots, table, coef, acc, small_sem, table_sem):
    blocks, per_block = screen.shape
    half, states, aux = coef_own.shape
    me = lax.axis_index(axis) % 2
    total = fetch(live_h, screen_h, table_h, live, screen, slots, table, small_sem, table_sem)
    acc[...] = jnp.zeros_like(acc)
    coef[0:half] = coef_own[...]
    coef[half : 2 * half] = coef_other[...]
    coef[2 * half] = jnp.zeros((states, aux), BF16)

    def chunk(c, _):
        results = []
        for p in range(PAIRS):
            i = c * PAIRS + p
            slot, b, t, rows = pair_at(i, slots, live, screen, total, 2 * half, own, half, me)

            @pl.when((t == 0) & (i < total))
            def _():
                block_copy(table_h, table, table_sem, live, b, per_block * aux, aux).wait()

            results.append((slot, b, rows))
        products = []
        for slot, b, rows in results:
            tile = table[pl.ds(pl.multiple_of(slot * aux, 2 * aux), 2 * aux), :]
            picked = jnp.concatenate([coef[rows[0]], coef[rows[1]]], axis=1)
            products.append(lax.dot_general(picked, tile, NN, preferred_element_type=F32))
        for (slot, b, rows), product in zip(results, products):
            acc[b] = acc[b] + product
        return 0

    lax.fori_loop(0, (total + PAIRS - 1) // PAIRS, chunk, 0)
    out[...] = acc[...].astype(out.dtype)


def metric_kernel(own, axis, gamma_own, gamma_other, metric, keep, send, high, low):
    half, states, aux = keep.shape
    rows = metric.shape[0]
    width = own * aux
    me = lax.axis_index(axis) % 2
    sides = [(gamma_own, keep, me), (gamma_other, send, 1 - me)]
    fitted = jnp.zeros((states, rows), F32)
    for chip in range(half // own):
        for gamma, _, side in sides:
            part = pl.ds(pl.multiple_of((chip * 2 + side) * width, width), width)
            whole = metric[:, part]
            h = whole.astype(BF16)
            l = (whole - h.astype(F32)).astype(BF16)
            high[:, part] = h
            low[:, part] = l
            g = jnp.concatenate([gamma[chip * own + k] for k in range(own)], axis=1)
            fitted += lax.dot_general(g, h, NT, preferred_element_type=F32)
            fitted += lax.dot_general(g, l, NT, preferred_element_type=F32)
    fitted_high = fitted.astype(BF16)
    fitted_low = (fitted - fitted_high.astype(F32)).astype(BF16)
    for chip in range(half // own):
        for _, out, side in sides:
            part = pl.ds(pl.multiple_of((chip * 2 + side) * width, width), width)
            h, l = high[:, part], low[:, part]
            c = lax.dot_general(fitted_high, h, NN, preferred_element_type=F32)
            c += lax.dot_general(fitted_high, l, NN, preferred_element_type=F32)
            c += lax.dot_general(fitted_low, h, NN, preferred_element_type=F32)
            for k in range(own):
                out[chip * own + k] = c[:, k * aux : (k + 1) * aux].astype(out.dtype)


def exchange(x, axis, devices, bit):
    return lax.ppermute(x, axis, [(j, j ^ bit) for j in range(devices)])


def summed(keep, send, axis, devices):
    total = keep + exchange(send, axis, devices, 1).astype(F32)
    bit = 2
    while bit < devices:
        total = total + exchange(total.astype(BF16), axis, devices, bit).astype(F32)
        bit *= 2
    return total


def per_device(devices, density, three_index, live, screen, metric_inverse):
    axis = "pair"
    blocks, per_block = screen.shape
    states = density.shape[1]
    aux, pairs = three_index.shape[2:]
    own = metric_inverse.shape[0] // aux
    half = metric_inverse.shape[1] // aux // 2
    table = three_index.reshape(blocks * per_block * aux, pairs)
    hbm = pl.BlockSpec(memory_space=pltpu.HBM)
    vmem = pl.BlockSpec(memory_space=pltpu.VMEM)
    lists = [
        pltpu.SMEM((blocks,), jnp.int32),
        pltpu.SMEM((blocks, per_block), jnp.int32),
        pltpu.SMEM((blocks * per_block // 2 + PAIRS,), jnp.int32),
    ]
    sems = [pltpu.SemaphoreType.DMA((3,)), pltpu.SemaphoreType.DMA((blocks,))]
    halves = (jax.ShapeDtypeStruct((half, states, aux), F32), jax.ShapeDtypeStruct((half, states, aux), F32))
    flops = 2 * blocks * per_block * aux * pairs * states

    keep, send = pl.pallas_call(
        functools.partial(gamma_kernel, own, axis),
        out_shape=halves,
        in_specs=[hbm] * 4,
        out_specs=(vmem, vmem),
        scratch_shapes=lists
        + [pltpu.VMEM(density.shape, BF16), pltpu.VMEM(table.shape, BF16), pltpu.VMEM((2 * half + 1, states, aux), F32)]
        + sems,
        compiler_params=pltpu.CompilerParams(vmem_limit_bytes=40 * MIB),
        cost_estimate=pl.CostEstimate(flops=flops, bytes_accessed=table.size * 2, transcendentals=0),
        name="gamma",
    )(live, screen, density, table)
    gamma = summed(keep, send, axis, devices).astype(BF16)
    gamma_other = exchange(gamma, axis, devices, 1)

    keep, send = pl.pallas_call(
        functools.partial(metric_kernel, own, axis),
        out_shape=halves,
        in_specs=[vmem] * 3,
        out_specs=(vmem, vmem),
        scratch_shapes=[pltpu.VMEM(metric_inverse.shape, BF16)] * 2,
        compiler_params=pltpu.CompilerParams(vmem_limit_bytes=24 * MIB),
        cost_estimate=pl.CostEstimate(flops=10 * metric_inverse.size * states, bytes_accessed=metric_inverse.size * 4, transcendentals=0),
        name="metric",
    )(gamma, gamma_other, metric_inverse)
    total = summed(keep, send, axis, devices)
    mine = (lax.axis_index(axis) // 2) * own
    coefficients = lax.dynamic_slice_in_dim(total, mine, own, axis=0)
    rounded = total.astype(BF16)
    rounded_other = exchange(rounded, axis, devices, 1)

    response = pl.pallas_call(
        functools.partial(response_kernel, own, axis),
        out_shape=jax.ShapeDtypeStruct(density.shape, BF16),
        in_specs=[hbm] * 3 + [vmem] * 2,
        out_specs=vmem,
        scratch_shapes=lists
        + [pltpu.VMEM(table.shape, BF16), pltpu.VMEM((2 * half + 1, states, aux), BF16), pltpu.VMEM(density.shape, F32)]
        + sems,
        compiler_params=pltpu.CompilerParams(vmem_limit_bytes=40 * MIB),
        cost_estimate=pl.CostEstimate(flops=flops, bytes_accessed=table.size * 2, transcendentals=0),
        name="response",
    )(live, screen, table, rounded, rounded_other)
    return (response, coefficients)


def solution(mesh):
    devices = mesh.shape["pair"]
    placed = (
        P(("groups", "pair"), None, None),
        P(("groups", "pair"), None, None, None),
        P(("groups", "pair")),
        P(("groups", "pair"), None),
        P("pair", None),
    )
    return jax.shard_map(
        functools.partial(per_device, devices),
        mesh=mesh,
        in_specs=placed,
        out_specs=(P(("groups", "pair"), None, None), P(("groups", "pair"), None, None)),
        check_vma=False,
    )
```

```python
import functools

import jax
import jax.numpy as jnp
from jax import lax
from jax.experimental import pallas as pl
from jax.experimental.pallas import tpu as pltpu
from jax.sharding import PartitionSpec as P

F32 = jnp.float32
BF16 = jnp.bfloat16
NT = (((1,), (1,)), ((), ()))
NN = (((1,), (0,)), ((), ()))
PAIRS = 8
HEAD = 4
MIB = 2**20


def divide(x, by):
    if by & (by - 1) == 0:
        return lax.shift_right_logical(x, by.bit_length() - 1), x & (by - 1)
    return lax.div(x, by), lax.rem(x, by)


def place(axis):
    index = lax.axis_index(axis)
    return index & 1, lax.shift_right_logical(index, 1) & 1


def row_of(a, own, quarter, first, second):
    owner, rest = divide(a, own)
    return (
        (((owner & 1) ^ first) * 2 + ((lax.shift_right_logical(owner, 1) & 1) ^ second)) * quarter
        + lax.shift_right_logical(owner, 2) * own
        + rest
    )


def list_tails(live, slots, blocks, per_block):
    def block(b, total):
        pairs = lax.shift_right_logical(live[b] + 1, 1)

        def one(p, total):
            slots[total] = b * per_block + 2 * p
            return total + 1

        return lax.fori_loop(HEAD, pairs, one, total)

    total = lax.fori_loop(0, blocks, block, 0)
    for p in range(PAIRS):
        slots[total + p] = 0
    return total


def describe(slot, valid, live, screen, dead, own, quarter, bits):
    b, t = divide(slot, screen.shape[1])
    rows = []
    for k in (0, 1):
        row = row_of(screen[b, t + k], own, quarter, *bits)
        ok = t + k < live[b]
        rows.append(jnp.where(ok if valid is None else ok & valid, row, dead))
    return slot, b, rows


def chunks(live, screen, slots, total, dead, own, quarter, bits, ready_heads, ready_tails, work):
    blocks, per_block = screen.shape
    step = PAIRS // HEAD

    def head(c, _):
        ready_heads(c * step, step)
        entries = []
        for p in range(PAIRS):
            slot = (c * step + p // HEAD) * per_block + 2 * (p % HEAD)
            entries.append(describe(slot, None, live, screen, dead, own, quarter, bits))
        work(entries)
        return 0

    lax.fori_loop(0, blocks // step, head, 0)

    def tail(c, waited):
        last, _ = divide(slots[jnp.minimum(c * PAIRS + PAIRS - 1, total - 1)], per_block)
        waited = ready_tails(waited, last + 1)
        entries = []
        for p in range(PAIRS):
            i = c * PAIRS + p
            entries.append(describe(slots[i], i < total, live, screen, dead, own, quarter, bits))
        work(entries)
        return waited

    lax.fori_loop(0, lax.shift_right_logical(total + PAIRS - 1, PAIRS.bit_length() - 1), tail, 0)


def gamma_kernel(own, axis, live_h, screen_h, density_h, table_h, near, far, table, live, screen, slots, density, acc, small_sem, head_sem, tail_sem):
    blocks, per_block = screen.shape
    half, states, aux = near.shape
    bits = place(axis)
    small = [
        pltpu.make_async_copy(live_h, live, small_sem.at[0]),
        pltpu.make_async_copy(screen_h, screen, small_sem.at[1]),
        pltpu.make_async_copy(density_h, density, small_sem.at[2]),
    ]
    for copy in small:
        copy.start()

    def head_copy(b):
        part = pl.ds(pl.multiple_of(b * per_block * aux, 2 * aux), 2 * HEAD * aux)
        return pltpu.make_async_copy(table_h.at[part], table.at[part], head_sem.at[b])

    def tail_copy(b):
        rows = (lax.shift_right_logical(live[b] + 1, 1) - HEAD) * (2 * aux)
        part = pl.ds(pl.multiple_of(b * per_block * aux + 2 * HEAD * aux, 2 * aux), pl.multiple_of(rows, 2 * aux))
        return pltpu.make_async_copy(table_h.at[part], table.at[part], tail_sem.at[b])

    for b in range(blocks):
        head_copy(b).start()
    small[0].wait()
    for b in range(blocks):

        @pl.when(live[b] > 2 * HEAD)
        def _():
            tail_copy(b).start()

    acc[...] = jnp.zeros_like(acc)
    total = list_tails(live, slots, blocks, per_block)
    small[1].wait()
    small[2].wait()

    def ready_heads(b, count):
        for k in range(count):
            head_copy(b + k).wait()

    def ready_tails(begin, end):
        def one(b, _):
            @pl.when(live[b] > 2 * HEAD)
            def _():
                tail_copy(b).wait()

            return 0

        lax.fori_loop(begin, end, one, 0)
        return jnp.maximum(begin, end)

    def work(entries):
        products = []
        for slot, b, _ in entries:
            tile = table[pl.ds(pl.multiple_of(slot * aux, 2 * aux), 2 * aux), :]
            products.append(lax.dot_general(density[b], tile, NT, preferred_element_type=F32))
        for (_, _, rows), product in zip(entries, products):
            for k in (0, 1):
                acc[rows[k]] = acc[rows[k]] + product[:, k * aux : (k + 1) * aux]

    chunks(live, screen, slots, total, 2 * half, own, half // 2, bits, ready_heads, ready_tails, work)
    near[...] = acc[0:half]
    far[...] = acc[half : 2 * half]


def response_kernel(own, axis, live_h, screen_h, table, *refs):
    coefs, (sums, out, mine, live, screen, slots, coef, acc, small_sem) = refs[:4], refs[4:]
    blocks, per_block = screen.shape
    quarter, states, aux = coefs[0].shape
    bits = place(axis)
    small = [
        pltpu.make_async_copy(live_h, live, small_sem.at[0]),
        pltpu.make_async_copy(screen_h, screen, small_sem.at[1]),
    ]
    for copy in small:
        copy.start()
    acc[...] = jnp.zeros_like(acc)
    mine[...] = sums[pl.ds(lax.shift_right_logical(lax.axis_index(axis), 2) * own, own)]
    for k in range(4):
        coef[k * quarter : (k + 1) * quarter] = coefs[k][...]
    coef[4 * quarter] = jnp.zeros((states, aux), BF16)
    small[0].wait()
    total = list_tails(live, slots, blocks, per_block)
    small[1].wait()

    def work(entries):
        products = []
        for slot, b, rows in entries:
            tile = table[pl.ds(pl.multiple_of(slot * aux, 2 * aux), 2 * aux), :]
            picked = jnp.concatenate([coef[rows[0]], coef[rows[1]]], axis=1)
            products.append(lax.dot_general(picked, tile, NN, preferred_element_type=F32))
        for (_, b, _), product in zip(entries, products):
            acc[b] = acc[b] + product

    chunks(live, screen, slots, total, 4 * quarter, own, quarter, bits, lambda b, count: None, lambda begin, end: end, work)
    out[...] = acc[...].astype(out.dtype)


def metric_kernel(own, axis, *refs):
    gammas, (metric, near, far, high, low) = refs[:4], refs[4:]
    quarter, states, aux = gammas[0].shape
    rows = metric.shape[0]
    width = own * aux
    first, second = place(axis)

    def columns(h, k):
        owner = (h * 2 + ((k & 1) ^ second)) * 2 + ((k >> 1) ^ first)
        return pl.ds(pl.multiple_of(owner * width, width), width)

    fitted = jnp.zeros((states, rows), F32)
    for h in range(quarter // own):
        for k in range(4):
            part = columns(h, k)
            whole = metric[:, part]
            m_high = whole.astype(BF16)
            m_low = (whole - m_high.astype(F32)).astype(BF16)
            high[:, part] = m_high
            low[:, part] = m_low
            g = jnp.concatenate([gammas[k][h * own + j] for j in range(own)], axis=1)
            fitted += lax.dot_general(g, m_high, NT, preferred_element_type=F32)
            fitted += lax.dot_general(g, m_low, NT, preferred_element_type=F32)
    fitted_high = fitted.astype(BF16)
    fitted_low = (fitted - fitted_high.astype(F32)).astype(BF16)
    both = jnp.concatenate([fitted_high, fitted_low], axis=0)
    for h in range(quarter // own):
        for k in range(4):
            part = columns(h, k)
            c = lax.dot_general(both, high[:, part], NN, preferred_element_type=F32)
            c = c[:states] + c[states:] + lax.dot_general(fitted_high, low[:, part], NN, preferred_element_type=F32)
            out = near if k < 2 else far
            for j in range(own):
                out[(k & 1) * quarter + h * own + j] = c[:, j * aux : (j + 1) * aux]


def exchange(x, axis, devices, bit):
    return lax.ppermute(x, axis, [(j, j ^ bit) for j in range(devices)])


def summed(near, far, axis, devices):
    quarter = near.shape[0] // 2
    total = near + exchange(far, axis, devices, 1)
    total = total[:quarter] + exchange(total[quarter:].astype(BF16), axis, devices, 2).astype(F32)
    bit = 4
    while bit < devices:
        total = total + exchange(total.astype(BF16), axis, devices, bit).astype(F32)
        bit *= 2
    return total


def quarters(mine, axis, devices):
    other = exchange(mine, axis, devices, 2)
    return mine, other, exchange(mine, axis, devices, 1), exchange(other, axis, devices, 1)


def per_device(devices, density, three_index, live, screen, metric_inverse):
    axis = "pair"
    blocks, per_block = screen.shape
    states = density.shape[1]
    aux, pairs = three_index.shape[2:]
    own = metric_inverse.shape[0] // aux
    half = metric_inverse.shape[1] // aux // 2
    table = three_index.reshape(blocks * per_block * aux, pairs)
    anywhere = pl.BlockSpec(memory_space=pl.ANY)
    vmem = pl.BlockSpec(memory_space=pltpu.VMEM)
    lists = [
        pltpu.SMEM((blocks,), jnp.int32),
        pltpu.SMEM((blocks, per_block), jnp.int32),
        pltpu.SMEM((blocks * per_block // 2 + PAIRS,), jnp.int32),
    ]
    in_hbm = lambda x: pltpu.with_memory_space_constraint(x, pltpu.HBM)
    live, screen = in_hbm(live), in_hbm(screen)
    halves = [pltpu.VMEM((half, states, aux), F32)] * 2
    flops = 2 * blocks * per_block * aux * pairs * states

    near, far, table = pl.pallas_call(
        functools.partial(gamma_kernel, own, axis),
        out_shape=(*halves, pltpu.VMEM(table.shape, BF16)),
        in_specs=[anywhere] * 4,
        out_specs=(vmem, vmem, vmem),
        scratch_shapes=lists
        + [
            pltpu.VMEM(density.shape, BF16),
            pltpu.VMEM((2 * half + 1, states, aux), F32),
            pltpu.SemaphoreType.DMA((3,)),
            pltpu.SemaphoreType.DMA((blocks,)),
            pltpu.SemaphoreType.DMA((blocks,)),
        ],
        compiler_params=pltpu.CompilerParams(vmem_limit_bytes=16 * MIB),
        cost_estimate=pl.CostEstimate(flops=flops, bytes_accessed=table.size * 2, transcendentals=0),
        name="gamma",
    )(live, screen, in_hbm(density), in_hbm(table))
    gammas = quarters(summed(near, far, axis, devices).astype(BF16), axis, devices)

    near, far = pl.pallas_call(
        functools.partial(metric_kernel, own, axis),
        out_shape=tuple(halves),
        in_specs=[vmem] * 5,
        out_specs=(vmem, vmem),
        scratch_shapes=[pltpu.VMEM(metric_inverse.shape, BF16)] * 2,
        compiler_params=pltpu.CompilerParams(vmem_limit_bytes=24 * MIB),
        cost_estimate=pl.CostEstimate(flops=10 * metric_inverse.size * states, bytes_accessed=metric_inverse.size * 4, transcendentals=0),
        name="metric",
    )(*gammas, metric_inverse)
    total = summed(near, far, axis, devices)
    rounded = quarters(total.astype(BF16), axis, devices)

    return pl.pallas_call(
        functools.partial(response_kernel, own, axis),
        out_shape=(jax.ShapeDtypeStruct(density.shape, BF16), jax.ShapeDtypeStruct((own, states, aux), F32)),
        in_specs=[anywhere] * 2 + [vmem] * 6,
        out_specs=(vmem, vmem),
        scratch_shapes=lists
        + [
            pltpu.VMEM((2 * half + 1, states, aux), BF16),
            pltpu.VMEM(density.shape, F32),
            pltpu.SemaphoreType.DMA((2,)),
        ],
        compiler_params=pltpu.CompilerParams(vmem_limit_bytes=16 * MIB),
        cost_estimate=pl.CostEstimate(flops=flops, bytes_accessed=table.size * 2, transcendentals=0),
        name="response",
    )(live, screen, pltpu.with_memory_space_constraint(table, pltpu.VMEM), *rounded, total)


def solution(mesh):
    devices = mesh.shape["pair"]
    placed = (
        P(("groups", "pair"), None, None),
        P(("groups", "pair"), None, None, None),
        P(("groups", "pair")),
        P(("groups", "pair"), None),
        P("pair", None),
    )
    return jax.shard_map(
        functools.partial(per_device, devices),
        mesh=mesh,
        in_specs=placed,
        out_specs=(P(("groups", "pair"), None, None), P(("groups", "pair"), None, None)),
        check_vma=False,
    )
```

```python
import functools

import jax
import jax.numpy as jnp
from jax import lax
from jax.experimental import pallas as pl
from jax.experimental.pallas import tpu as pltpu
from jax.sharding import PartitionSpec as P

F32 = jnp.float32
BF16 = jnp.bfloat16
NT = (((1,), (1,)), ((), ()))
NN = (((1,), (0,)), ((), ()))
PAIRS = 32
LEAST = 8
HEAD = 4
MIB = 2**20


def divide(x, by):
    if by & (by - 1) == 0:
        return lax.shift_right_logical(x, by.bit_length() - 1), x & (by - 1)
    return lax.div(x, by), lax.rem(x, by)


def place(axis):
    index = lax.axis_index(axis)
    return index & 1, lax.shift_right_logical(index, 1) & 1


def row_of(a, own, quarter, first, second):
    owner, rest = divide(a, own)
    return (
        (((owner & 1) ^ first) * 2 + ((lax.shift_right_logical(owner, 1) & 1) ^ second)) * quarter
        + lax.shift_right_logical(owner, 2) * own
        + rest
    )


def list_tails(live, slots, blocks, per_block):
    def block(b, total):
        pairs = lax.shift_right_logical(live[b] + 1, 1)

        def one(p, total):
            slots[total] = b * per_block + 2 * p
            return total + 1

        return lax.fori_loop(HEAD, pairs, one, total)

    total = lax.fori_loop(0, blocks, block, 0)
    for p in range(PAIRS):
        slots[total + p] = 0
    return total


def describe(slot, valid, live, screen, dead, own, quarter, bits):
    b, t = divide(slot, screen.shape[1])
    rows = []
    for k in (0, 1):
        row = row_of(screen[b, t + k], own, quarter, *bits)
        ok = t + k < live[b]
        rows.append(jnp.where(ok if valid is None else ok & valid, row, dead))
    return slot, b, rows


def chunks(live, screen, slots, total, dead, own, quarter, bits, ready_heads, ready_tails, work):
    blocks, per_block = screen.shape
    step = max(1, min(blocks, PAIRS // HEAD))

    def head(c, _):
        ready_heads(c * step, step)
        entries = []
        for p in range(step * HEAD):
            slot = (c * step + p // HEAD) * per_block + 2 * (p % HEAD)
            entries.append(describe(slot, None, live, screen, dead, own, quarter, bits))
        work(entries)
        return 0

    lax.fori_loop(0, blocks // step, head, 0)

    def tail(size, begin, waited):
        last, _ = divide(slots[jnp.minimum(begin + size - 1, total - 1)], per_block)
        waited = ready_tails(waited, last + 1)
        entries = []
        for p in range(size):
            i = begin + p
            entries.append(describe(slots[i], i < total, live, screen, dead, own, quarter, bits))
        work(entries)
        return waited

    whole = lax.shift_right_logical(total, PAIRS.bit_length() - 1)
    waited = lax.fori_loop(0, whole, lambda c, waited: tail(PAIRS, c * PAIRS, waited), 0)
    begin, size = whole * PAIRS, PAIRS // 2
    while size >= LEAST:
        left = total - begin
        if size > LEAST:
            more = (left >= size).astype(jnp.int32)
        else:
            more = lax.div(left + size - 1, size)
        waited = lax.fori_loop(0, more, lambda c, waited, begin=begin, size=size: tail(size, begin + c * size, waited), waited)
        begin = begin + more * size
        size //= 2

def gamma_kernel(own, axis, live_h, screen_h, density_h, table_h, near, far, table, live, screen, slots, density, acc, small_sem, head_sem, tail_sem):
    blocks, per_block = screen.shape
    half, states, aux = near.shape
    bits = place(axis)
    small = [
        pltpu.make_async_copy(live_h, live, small_sem.at[0]),
        pltpu.make_async_copy(screen_h, screen, small_sem.at[1]),
        pltpu.make_async_copy(density_h, density, small_sem.at[2]),
    ]
    for copy in small:
        copy.start()

    def head_copy(b):
        part = pl.ds(pl.multiple_of(b * per_block * aux, 2 * aux), 2 * HEAD * aux)
        return pltpu.make_async_copy(table_h.at[part], table.at[part], head_sem.at[b])

    def tail_copy(b):
        rows = (lax.shift_right_logical(live[b] + 1, 1) - HEAD) * (2 * aux)
        part = pl.ds(pl.multiple_of(b * per_block * aux + 2 * HEAD * aux, 2 * aux), pl.multiple_of(rows, 2 * aux))
        return pltpu.make_async_copy(table_h.at[part], table.at[part], tail_sem.at[b])

    for b in range(blocks):
        head_copy(b).start()
    small[0].wait()
    for b in range(blocks):

        @pl.when(live[b] > 2 * HEAD)
        def _():
            tail_copy(b).start()

    acc[...] = jnp.zeros_like(acc)
    total = list_tails(live, slots, blocks, per_block)
    small[1].wait()
    small[2].wait()

    def ready_heads(b, count):
        for k in range(count):
            head_copy(b + k).wait()

    def ready_tails(begin, end):
        def one(b, _):
            @pl.when(live[b] > 2 * HEAD)
            def _():
                tail_copy(b).wait()

            return 0

        lax.fori_loop(begin, end, one, 0)
        return jnp.maximum(begin, end)

    def work(entries):
        products = []
        for slot, b, _ in entries:
            tile = table[pl.ds(pl.multiple_of(slot * aux, 2 * aux), 2 * aux), :]
            products.append(lax.dot_general(density[b], tile, NT, preferred_element_type=F32))
        for (_, _, rows), product in zip(entries, products):
            for k in (0, 1):
                acc[rows[k]] = acc[rows[k]] + product[:, k * aux : (k + 1) * aux]

    chunks(live, screen, slots, total, 2 * half, own, half // 2, bits, ready_heads, ready_tails, work)
    near[...] = acc[0:half]
    far[...] = acc[half : 2 * half]


def response_kernel(own, axis, live_h, screen_h, table, *refs):
    coefs, (sums, out, mine, live, screen, slots, coef, acc, small_sem) = refs[:4], refs[4:]
    blocks, per_block = screen.shape
    quarter, states, aux = coefs[0].shape
    bits = place(axis)
    small = [
        pltpu.make_async_copy(live_h, live, small_sem.at[0]),
        pltpu.make_async_copy(screen_h, screen, small_sem.at[1]),
    ]
    for copy in small:
        copy.start()
    acc[...] = jnp.zeros_like(acc)
    mine[...] = sums[pl.ds(lax.shift_right_logical(lax.axis_index(axis), 2) * own, own)]
    for k in range(4):
        coef[k * quarter : (k + 1) * quarter] = coefs[k][...]
    coef[4 * quarter] = jnp.zeros((states, aux), BF16)
    small[0].wait()
    total = list_tails(live, slots, blocks, per_block)
    small[1].wait()

    def work(entries):
        products = []
        for slot, b, rows in entries:
            tile = table[pl.ds(pl.multiple_of(slot * aux, 2 * aux), 2 * aux), :]
            picked = jnp.concatenate([coef[rows[0]], coef[rows[1]]], axis=1)
            products.append(lax.dot_general(picked, tile, NN, preferred_element_type=F32))
        for (_, b, _), product in zip(entries, products):
            acc[b] = acc[b] + product

    chunks(live, screen, slots, total, 4 * quarter, own, quarter, bits, lambda b, count: None, lambda begin, end: end, work)
    out[...] = acc[...].astype(out.dtype)


def metric_kernel(own, axis, *refs):
    gammas, (metric, near, far, high, low) = refs[:4], refs[4:]
    quarter, states, aux = gammas[0].shape
    rows = metric.shape[0]
    width = own * aux
    first, second = place(axis)

    def columns(h, k):
        owner = (h * 2 + ((k & 1) ^ second)) * 2 + ((k >> 1) ^ first)
        return pl.ds(pl.multiple_of(owner * width, width), width)

    fitted = jnp.zeros((states, rows), F32)
    for h in range(quarter // own):
        for k in range(4):
            part = columns(h, k)
            whole = metric[:, part]
            m_high = whole.astype(BF16)
            m_low = (whole - m_high.astype(F32)).astype(BF16)
            high[:, part] = m_high
            low[:, part] = m_low
            g = jnp.concatenate([gammas[k][h * own + j] for j in range(own)], axis=1)
            fitted += lax.dot_general(g, m_high, NT, preferred_element_type=F32)
            fitted += lax.dot_general(g, m_low, NT, preferred_element_type=F32)
    fitted_high = fitted.astype(BF16)
    fitted_low = (fitted - fitted_high.astype(F32)).astype(BF16)
    both = jnp.concatenate([fitted_high, fitted_low], axis=0)
    for h in range(quarter // own):
        for k in range(4):
            part = columns(h, k)
            c = lax.dot_general(both, high[:, part], NN, preferred_element_type=F32)
            c = c[:states] + c[states:] + lax.dot_general(fitted_high, low[:, part], NN, preferred_element_type=F32)
            out = near if k < 2 else far
            for j in range(own):
                out[(k & 1) * quarter + h * own + j] = c[:, j * aux : (j + 1) * aux]


def exchange(x, axis, devices, bit):
    return lax.ppermute(x, axis, [(j, j ^ bit) for j in range(devices)])


def summed(near, far, axis, devices):
    quarter = near.shape[0] // 2
    total = near + exchange(far, axis, devices, 1)
    total = total[:quarter] + exchange(total[quarter:].astype(BF16), axis, devices, 2).astype(F32)
    bit = 4
    while bit < devices:
        total = total + exchange(total.astype(BF16), axis, devices, bit).astype(F32)
        bit *= 2
    return total


def quarters(mine, axis, devices):
    other = exchange(mine, axis, devices, 2)
    return mine, other, exchange(mine, axis, devices, 1), exchange(other, axis, devices, 1)


def per_device(devices, density, three_index, live, screen, metric_inverse):
    axis = "pair"
    blocks, per_block = screen.shape
    states = density.shape[1]
    aux, pairs = three_index.shape[2:]
    own = metric_inverse.shape[0] // aux
    half = metric_inverse.shape[1] // aux // 2
    table = three_index.reshape(blocks * per_block * aux, pairs)
    anywhere = pl.BlockSpec(memory_space=pl.ANY)
    vmem = pl.BlockSpec(memory_space=pltpu.VMEM)
    lists = [
        pltpu.SMEM((blocks,), jnp.int32),
        pltpu.SMEM((blocks, per_block), jnp.int32),
        pltpu.SMEM((blocks * per_block // 2 + PAIRS,), jnp.int32),
    ]
    in_hbm = lambda x: pltpu.with_memory_space_constraint(x, pltpu.HBM)
    halves = [pltpu.VMEM((half, states, aux), F32)] * 2
    flops = 2 * blocks * per_block * aux * pairs * states

    near, far, table = pl.pallas_call(
        functools.partial(gamma_kernel, own, axis),
        out_shape=(*halves, pltpu.VMEM(table.shape, BF16)),
        in_specs=[anywhere] * 4,
        out_specs=(vmem, vmem, vmem),
        scratch_shapes=lists
        + [
            pltpu.VMEM(density.shape, BF16),
            pltpu.VMEM((2 * half + 1, states, aux), F32),
            pltpu.SemaphoreType.DMA((3,)),
            pltpu.SemaphoreType.DMA((blocks,)),
            pltpu.SemaphoreType.DMA((blocks,)),
        ],
        compiler_params=pltpu.CompilerParams(vmem_limit_bytes=16 * MIB),
        cost_estimate=pl.CostEstimate(flops=flops, bytes_accessed=table.size * 2, transcendentals=0),
        name="gamma",
    )(in_hbm(live), in_hbm(screen), in_hbm(density), in_hbm(table))
    gammas = quarters(summed(near, far, axis, devices).astype(BF16), axis, devices)

    near, far = pl.pallas_call(
        functools.partial(metric_kernel, own, axis),
        out_shape=tuple(halves),
        in_specs=[vmem] * 5,
        out_specs=(vmem, vmem),
        scratch_shapes=[pltpu.VMEM(metric_inverse.shape, BF16)] * 2,
        compiler_params=pltpu.CompilerParams(vmem_limit_bytes=24 * MIB),
        cost_estimate=pl.CostEstimate(flops=10 * metric_inverse.size * states, bytes_accessed=metric_inverse.size * 4, transcendentals=0),
        name="metric",
    )(*gammas, metric_inverse)
    total = summed(near, far, axis, devices)
    rounded = quarters(total.astype(BF16), axis, devices)

    return pl.pallas_call(
        functools.partial(response_kernel, own, axis),
        out_shape=(jax.ShapeDtypeStruct(density.shape, BF16), jax.ShapeDtypeStruct((own, states, aux), F32)),
        in_specs=[anywhere] * 2 + [vmem] * 6,
        out_specs=(vmem, vmem),
        scratch_shapes=lists
        + [
            pltpu.VMEM((2 * half + 1, states, aux), BF16),
            pltpu.VMEM(density.shape, F32),
            pltpu.SemaphoreType.DMA((2,)),
        ],
        compiler_params=pltpu.CompilerParams(vmem_limit_bytes=16 * MIB),
        cost_estimate=pl.CostEstimate(flops=flops, bytes_accessed=table.size * 2, transcendentals=0),
        name="response",
    )(live, screen, pltpu.with_memory_space_constraint(table, pltpu.VMEM), *rounded, total)


def solution(mesh):
    devices = mesh.shape["pair"]
    placed = (
        P(("groups", "pair"), None, None),
        P(("groups", "pair"), None, None, None),
        P(("groups", "pair")),
        P(("groups", "pair"), None),
        P("pair", None),
    )
    return jax.shard_map(
        functools.partial(per_device, devices),
        mesh=mesh,
        in_specs=placed,
        out_specs=(P(("groups", "pair"), None, None), P(("groups", "pair"), None, None)),
        check_vma=False,
    )
```

```python
import functools

import jax
import jax.numpy as jnp
from jax import lax
from jax.experimental import pallas as pl
from jax.experimental.pallas import tpu as pltpu
from jax.sharding import PartitionSpec as P

F32 = jnp.float32
BF16 = jnp.bfloat16
NT = (((1,), (1,)), ((), ()))
NN = (((1,), (0,)), ((), ()))
PAIRS = 32
LEAST = 8
HEAD = 4
MIB = 2**20


def divide(x, by):
    if by & (by - 1) == 0:
        return lax.shift_right_logical(x, by.bit_length() - 1), x & (by - 1)
    return lax.div(x, by), lax.rem(x, by)


def place(axis):
    index = lax.axis_index(axis)
    return index & 1, lax.shift_right_logical(index, 1) & 1


def row_of(a, own, quarter, first, second):
    owner, rest = divide(a, own)
    return (
        (((owner & 1) ^ first) * 2 + ((lax.shift_right_logical(owner, 1) & 1) ^ second)) * quarter
        + lax.shift_right_logical(owner, 2) * own
        + rest
    )


def list_tails(live, slots, blocks, per_block):
    def block(b, total):
        pairs = lax.shift_right_logical(live[b] + 1, 1)

        def one(p, total):
            slots[total] = b * per_block + 2 * p
            return total + 1

        return lax.fori_loop(HEAD, pairs, one, total)

    total = lax.fori_loop(0, blocks, block, 0)
    for p in range(PAIRS):
        slots[total + p] = 0
    return total


def describe(slot, valid, live, screen, dead, own, quarter, bits):
    b, t = divide(slot, screen.shape[1])
    rows = []
    for k in (0, 1):
        row = row_of(screen[b, t + k], own, quarter, *bits)
        ok = t + k < live[b]
        rows.append(jnp.where(ok if valid is None else ok & valid, row, dead))
    return slot, b, rows


def rounds(total, state, work):
    whole = lax.shift_right_logical(total, PAIRS.bit_length() - 1)
    state = lax.fori_loop(0, whole, lambda c, state: work(PAIRS, c * PAIRS, state), state)
    begin, size = whole * PAIRS, PAIRS // 2
    while size >= LEAST:
        left = total - begin
        if size > LEAST:
            more = (left >= size).astype(jnp.int32)
        else:
            more = lax.div(left + size - 1, size)
        state = lax.fori_loop(0, more, lambda c, state, begin=begin, size=size: work(size, begin + c * size, state), state)
        begin = begin + more * size
        size //= 2
    return state


def chunks(live, screen, slots, total, dead, own, quarter, bits, ready_heads, ready_tails, work):
    blocks, per_block = screen.shape
    step = max(1, min(blocks, PAIRS // HEAD))

    def head(c, _):
        ready_heads(c * step, step)
        entries = []
        for p in range(step * HEAD):
            slot = (c * step + p // HEAD) * per_block + 2 * (p % HEAD)
            entries.append(describe(slot, None, live, screen, dead, own, quarter, bits))
        work(entries)
        return 0

    lax.fori_loop(0, blocks // step, head, 0)

    def tail(size, begin, waited):
        last, _ = divide(slots[jnp.minimum(begin + size - 1, total - 1)], per_block)
        waited = ready_tails(waited, last + 1)
        entries = []
        for p in range(size):
            i = begin + p
            entries.append(describe(slots[i], i < total, live, screen, dead, own, quarter, bits))
        work(entries)
        return waited

    rounds(total, 0, tail)


def gamma_kernel(own, axis, live_h, screen_h, density_h, table_h, near, far, table, live, screen, slots, density, acc, small_sem, head_sem, tail_sem):
    blocks, per_block = screen.shape
    half, states, aux = near.shape
    bits = place(axis)
    small = [
        pltpu.make_async_copy(live_h, live, small_sem.at[0]),
        pltpu.make_async_copy(screen_h, screen, small_sem.at[1]),
        pltpu.make_async_copy(density_h, density, small_sem.at[2]),
    ]
    for copy in small:
        copy.start()

    def head_copy(b):
        part = pl.ds(pl.multiple_of(b * per_block * aux, 2 * aux), 2 * HEAD * aux)
        return pltpu.make_async_copy(table_h.at[part], table.at[part], head_sem.at[b])

    def tail_copy(b):
        rows = (lax.shift_right_logical(live[b] + 1, 1) - HEAD) * (2 * aux)
        part = pl.ds(pl.multiple_of(b * per_block * aux + 2 * HEAD * aux, 2 * aux), pl.multiple_of(rows, 2 * aux))
        return pltpu.make_async_copy(table_h.at[part], table.at[part], tail_sem.at[b])

    for b in range(blocks):
        head_copy(b).start()
    small[0].wait()
    for b in range(blocks):

        @pl.when(live[b] > 2 * HEAD)
        def _():
            tail_copy(b).start()

    acc[...] = jnp.zeros_like(acc)
    total = list_tails(live, slots, blocks, per_block)
    small[1].wait()
    small[2].wait()

    def ready_heads(b, count):
        for k in range(count):
            head_copy(b + k).wait()

    def ready_tails(begin, end):
        def one(b, _):
            @pl.when(live[b] > 2 * HEAD)
            def _():
                tail_copy(b).wait()

            return 0

        lax.fori_loop(begin, end, one, 0)
        return jnp.maximum(begin, end)

    def work(entries):
        products = []
        for slot, b, _ in entries:
            tile = table[pl.ds(pl.multiple_of(slot * aux, 2 * aux), 2 * aux), :]
            products.append(lax.dot_general(density[b], tile, NT, preferred_element_type=F32))
        for (_, _, rows), product in zip(entries, products):
            for k in (0, 1):
                acc[rows[k]] = acc[rows[k]] + product[:, k * aux : (k + 1) * aux]

    chunks(live, screen, slots, total, 2 * half, own, half // 2, bits, ready_heads, ready_tails, work)
    near[...] = acc[0:half]
    far[...] = acc[half : 2 * half]


def plan_size(blocks, per_block):
    return blocks * per_block + 2 * LEAST + 1


def plan_kernel(own, axis, quarter, base, live_h, screen_h, plan, live, screen, sem):
    blocks, per_block = screen.shape
    size = plan_size(blocks, per_block)
    first, second = place(axis)
    small = [pltpu.make_async_copy(live_h, live, sem.at[0]), pltpu.make_async_copy(screen_h, screen, sem.at[1])]
    for copy in small:
        copy.start()
    for copy in small:
        copy.wait()
    dead = 2 * quarter

    def block(b, counts):
        def one(t, counts):
            mine, other = counts
            owner, rest = divide(screen[b, t], own)
            side = (lax.shift_right_logical(owner, 1) & 1) ^ second
            row = ((owner & 1) ^ first) * quarter + lax.shift_right_logical(owner, 2) * own + rest
            plan[jnp.where(side == 0, mine, size + other)] = (b * per_block + t) * base + row
            return mine + 1 - side, other + side

        mine, other = lax.fori_loop(0, live[b], one, counts)
        plan[mine] = b * per_block * base + dead
        plan[size + other] = b * per_block * base + dead
        return mine + (mine & 1), other + (other & 1)

    counts = lax.fori_loop(0, blocks, block, (0, 0))
    for k in (0, 1):
        for p in range(2 * LEAST):
            plan[k * size + counts[k] + p] = dead
        plan[(k + 1) * size - 1] = counts[k]


def add_responses(side, per_block, base, plan, table, coefs, coef, acc):
    quarter, states, aux = coefs[0].shape
    size = plan.shape[0] // 2
    for k in (0, 1):
        coef[k * quarter : (k + 1) * quarter] = coefs[k][...]
    coef[2 * quarter] = jnp.zeros((states, aux), BF16)

    def work(count, begin, state):
        products = []
        for p in range(count):
            entries = [divide(plan[side * size + 2 * (begin + p) + k], base) for k in (0, 1)]
            tiles = [table[pl.ds(pl.multiple_of(slot * aux, aux), aux), :] for slot, _ in entries]
            picked = jnp.concatenate([coef[row] for _, row in entries], axis=1)
            product = lax.dot_general(picked, jnp.concatenate(tiles, axis=0), NN, preferred_element_type=F32)
            products.append((divide(entries[0][0], per_block)[0], product))
        for b, product in products:
            acc[b] = acc[b] + product
        return state

    rounds(lax.shift_right_logical(plan[(side + 1) * size - 1], 1), 0, work)


def first_response_kernel(per_block, base, plan, table, coef_a, coef_b, acc, coef):
    acc[...] = jnp.zeros_like(acc)
    add_responses(0, per_block, base, plan, table, (coef_a, coef_b), coef, acc)


def second_response_kernel(per_block, base, own, axis, plan, table, coef_a, coef_b, before, sums, out, mine, coef, acc):
    mine[...] = sums[pl.ds(lax.shift_right_logical(lax.axis_index(axis), 2) * own, own)]
    acc[...] = before[...]
    add_responses(1, per_block, base, plan, table, (coef_a, coef_b), coef, acc)
    out[...] = acc[...].astype(out.dtype)


def columns(h, k, width, axis):
    first, second = place(axis)
    owner = (h * 2 + ((k & 1) ^ second)) * 2 + ((k >> 1) ^ first)
    return pl.ds(pl.multiple_of(owner * width, width), width)


def fit(own, axis, sides, gammas, high, low, fitted):
    quarter, _, aux = gammas[0].shape
    for h in range(quarter // own):
        for k, gamma in zip(sides, gammas):
            part = columns(h, k, own * aux, axis)
            g = jnp.concatenate([gamma[h * own + j] for j in range(own)], axis=1)
            fitted += lax.dot_general(g, high[:, part], NT, preferred_element_type=F32)
            fitted += lax.dot_general(g, low[:, part], NT, preferred_element_type=F32)
    return fitted


def spread(own, axis, sides, both, high, low, out):
    half, states, aux = out.shape
    for h in range(half // 2 // own):
        for k in sides:
            part = columns(h, k, own * aux, axis)
            c = lax.dot_general(both, high[:, part], NN, preferred_element_type=F32)
            c = c[:states] + c[states:] + lax.dot_general(both[:states], low[:, part], NN, preferred_element_type=F32)
            for j in range(own):
                out[(k & 1) * (half // 2) + h * own + j] = c[:, j * aux : (j + 1) * aux]


def first_metric_kernel(own, axis, gamma_a, gamma_b, metric, fitted, high, low):
    width = own * gamma_a.shape[2]
    for c in range(metric.shape[1] // width):
        part = slice(c * width, (c + 1) * width)
        whole = metric[:, part]
        m_high = whole.astype(BF16)
        high[:, part] = m_high
        low[:, part] = (whole - m_high.astype(F32)).astype(BF16)
    fitted[...] = fit(own, axis, (0, 2), (gamma_a, gamma_b), high, low, jnp.zeros(fitted.shape, F32))


def second_metric_kernel(own, axis, gamma_a, gamma_b, before, high, low, far, both):
    fitted = fit(own, axis, (1, 3), (gamma_a, gamma_b), high, low, before[...])
    fitted_high = fitted.astype(BF16)
    fitted_low = (fitted - fitted_high.astype(F32)).astype(BF16)
    both[...] = jnp.concatenate([fitted_high, fitted_low], axis=0)
    spread(own, axis, (2, 3), both[...], high, low, far)


def third_metric_kernel(own, axis, both, high, low, near):
    spread(own, axis, (0, 1), both[...], high, low, near)


def exchange(x, axis, devices, bit):
    return lax.ppermute(x, axis, [(j, j ^ bit) for j in range(devices)])


def summed(near, far, axis, devices, inputs=(), aside=None):
    quarter = near.shape[0] // 2
    total = near + exchange(far, axis, devices, 1)
    result = None
    if aside is None:
        got = exchange(total[quarter:].astype(BF16), axis, devices, 2)
    else:
        total, *inputs = lax.optimization_barrier((total, *inputs))
        got, result = lax.optimization_barrier((exchange(total[quarter:].astype(BF16), axis, devices, 2), aside(*inputs)))
    total = total[:quarter] + got.astype(F32)
    bit = 4
    while bit < devices:
        total = total + exchange(total.astype(BF16), axis, devices, bit).astype(F32)
        bit *= 2
    return total, result


def quarters(mine, axis, devices, aside=None):
    other = exchange(mine, axis, devices, 2)
    near = exchange(mine, axis, devices, 1)
    result = None
    if aside is not None:
        other, result = lax.optimization_barrier((other, aside(mine, near)))
    return (mine, other, near, exchange(other, axis, devices, 1)), result


def per_device(devices, density, three_index, live, screen, metric_inverse):
    axis = "pair"
    blocks, per_block = screen.shape
    states = density.shape[1]
    aux, pairs = three_index.shape[2:]
    own = metric_inverse.shape[0] // aux
    half = metric_inverse.shape[1] // aux // 2
    table = three_index.reshape(blocks * per_block * aux, pairs)
    anywhere = pl.BlockSpec(memory_space=pl.ANY)
    vmem = pl.BlockSpec(memory_space=pltpu.VMEM)
    lists = [
        pltpu.SMEM((blocks,), jnp.int32),
        pltpu.SMEM((blocks, per_block), jnp.int32),
        pltpu.SMEM((blocks * per_block // 2 + PAIRS,), jnp.int32),
    ]
    in_hbm = lambda x: pltpu.with_memory_space_constraint(x, pltpu.HBM)
    halves = [pltpu.VMEM((half, states, aux), F32)] * 2
    flops = 2 * blocks * per_block * aux * pairs * states

    near, far, table = pl.pallas_call(
        functools.partial(gamma_kernel, own, axis),
        out_shape=(*halves, pltpu.VMEM(table.shape, BF16)),
        in_specs=[anywhere] * 4,
        out_specs=(vmem, vmem, vmem),
        scratch_shapes=lists
        + [
            pltpu.VMEM(density.shape, BF16),
            pltpu.VMEM((2 * half + 1, states, aux), F32),
            pltpu.SemaphoreType.DMA((3,)),
            pltpu.SemaphoreType.DMA((blocks,)),
            pltpu.SemaphoreType.DMA((blocks,)),
        ],
        compiler_params=pltpu.CompilerParams(vmem_limit_bytes=16 * MIB),
        cost_estimate=pl.CostEstimate(flops=flops, bytes_accessed=table.size * 2, transcendentals=0),
        name="gamma",
    )(in_hbm(live), in_hbm(screen), in_hbm(density), in_hbm(table))
    quarter = half // 2
    base = 1 << (2 * quarter).bit_length()
    smem = pl.BlockSpec(memory_space=pltpu.SMEM)
    make_plan = pl.pallas_call(
        functools.partial(plan_kernel, own, axis, quarter, base),
        out_shape=jax.ShapeDtypeStruct((2 * plan_size(blocks, per_block),), jnp.int32),
        in_specs=[anywhere] * 2,
        out_specs=smem,
        scratch_shapes=lists[:2] + [pltpu.SemaphoreType.DMA((2,))],
        compiler_params=pltpu.CompilerParams(vmem_limit_bytes=MIB),
        cost_estimate=pl.CostEstimate(flops=0, bytes_accessed=6 * MIB, transcendentals=0),
        name="plan",
    )
    gamma, plan = summed(near, far, axis, devices, (live, screen), make_plan)
    params = pltpu.CompilerParams(vmem_limit_bytes=16 * MIB)
    rows = metric_inverse.shape[0]
    terms = [pltpu.VMEM(metric_inverse.shape, BF16)] * 2
    cost = pl.CostEstimate(flops=2 * metric_inverse.size * states, bytes_accessed=metric_inverse.size, transcendentals=0)
    first_metric = pl.pallas_call(
        functools.partial(first_metric_kernel, own, axis),
        out_shape=(pltpu.VMEM((states, rows), F32), *terms),
        in_specs=[vmem] * 3,
        out_specs=(vmem,) * 3,
        compiler_params=params,
        cost_estimate=cost,
        name="metric_first",
    )
    gammas, (before, *terms) = quarters(gamma.astype(BF16), axis, devices, lambda a, b: first_metric(a, b, metric_inverse))
    terms = [pltpu.with_memory_space_constraint(x, pltpu.VMEM) for x in terms]
    far, both = pl.pallas_call(
        functools.partial(second_metric_kernel, own, axis),
        out_shape=(halves[0], pltpu.VMEM((2 * states, rows), BF16)),
        in_specs=[vmem] * 5,
        out_specs=(vmem,) * 2,
        compiler_params=params,
        cost_estimate=cost,
        name="metric_second",
    )(gammas[1], gammas[3], before, *terms)
    near = pl.pallas_call(
        functools.partial(third_metric_kernel, own, axis),
        out_shape=halves[0],
        in_specs=[vmem] * 3,
        out_specs=vmem,
        compiler_params=params,
        cost_estimate=cost,
        name="metric_third",
    )(both, *terms)
    total, _ = summed(near, far, axis, devices)

    table = pltpu.with_memory_space_constraint(table, pltpu.VMEM)
    spare = pltpu.VMEM((half + 1, states, aux), BF16)
    cost = pl.CostEstimate(flops=flops // 2, bytes_accessed=table.size, transcendentals=0)
    first_response = pl.pallas_call(
        functools.partial(first_response_kernel, per_block, base),
        out_shape=pltpu.VMEM(density.shape, F32),
        in_specs=[smem] + [vmem] * 3,
        out_specs=vmem,
        scratch_shapes=[spare],
        compiler_params=params,
        cost_estimate=cost,
        name="response_first",
    )
    rounded, before = quarters(total.astype(BF16), axis, devices, lambda a, b: first_response(plan, table, a, b))
    return pl.pallas_call(
        functools.partial(second_response_kernel, per_block, base, own, axis),
        out_shape=(jax.ShapeDtypeStruct(density.shape, BF16), jax.ShapeDtypeStruct((own, states, aux), F32)),
        in_specs=[smem] + [vmem] * 5,
        out_specs=(vmem, vmem),
        scratch_shapes=[spare, pltpu.VMEM(density.shape, F32)],
        compiler_params=params,
        cost_estimate=cost,
        name="response_second",
    )(plan, table, rounded[1], rounded[3], before, total)


def solution(mesh):
    devices = mesh.shape["pair"]
    placed = (
        P(("groups", "pair"), None, None),
        P(("groups", "pair"), None, None, None),
        P(("groups", "pair")),
        P(("groups", "pair"), None),
        P("pair", None),
    )
    return jax.shard_map(
        functools.partial(per_device, devices),
        mesh=mesh,
        in_specs=placed,
        out_specs=(P(("groups", "pair"), None, None), P(("groups", "pair"), None, None)),
        check_vma=False,
    )
```
